32 devices in a mesh: visit: 4 (over y, core), patch: 8 (over z, x).
Axes of the slice: x: 2, y: 2, z: 4, core: 2. Of those that a mesh axis runs over, the one named last changes fastest.
Arguments:
- pieces: float32 [256, 512, 512], P(('visit', 'patch')), may hold values from -60 to 60
- ref_patch: float32 [8, 512, 512], P('patch', 'visit'), may hold values from -6 to 6
- piece_patch: int32 [256], P(('visit', 'patch')), may hold values from 0 to 7, as said below
- piece_visit: int32 [256], P(('visit', 'patch')), may hold values from 0 to 3, as said below
- anchors: int32 [256, 2], P(('visit', 'patch')), may hold values from 0 to 3584
- shifts: int32 [256, 2], P(('visit', 'patch')), may hold values from -2 to 2
- phases: float32 [256, 2], P(('visit', 'patch')), may hold values from 0 to 1
Outputs:
- matched: float32 [256, 512, 512], P(('visit', 'patch'))
- coefficients: float32 [16, 17, 17], P('visit')
The draws below stay inside these ranges and needn't reach their ends.
Inputs may be any that keep to these rules, and one draw needn't show every extreme that they name: `piece_patch`: among the 8 pieces of one device at most 2 name the same patch; for each index of the visit axis one patch, drawn from the seed, is named by exactly 2 pieces of every device of that index. `piece_visit`: among the 8 pieces of one device each value occurs exactly 8 / 4 times.
All inputs are finite; a program needn't handle non-finite values.
Results may differ from the reference program's by a relative error of at most 0.0003.
Values sent between devices are 32-bit elements; how exact they have to be, the bound alone decides.
A program may use at most 192 MiB of HBM per device.

```python
import jax
import jax.numpy as jnp
from jax import lax

PIX = 512
PIECE_DEV = 8
VIS_DEV = 4
CAP = 2
TERMS = 17
TILE = 4096
PATCHES = 8
VISITS = 16
PIECES = 256


def visit_layout(key):
    base_key = jax.random.fold_in(key, 7101)
    block_total = PIECES // PIECE_DEV

    def one_block(block_id):
        sub_key = jax.random.fold_in(base_key, block_id)
        ordering = jax.random.permutation(sub_key, PIECE_DEV)
        return (ordering % VIS_DEV).astype(jnp.int32)
    return jax.vmap(one_block)(jnp.arange(block_total, dtype=jnp.int32)).reshape(PIECES).astype(jnp.int32)


def draw_piece_visit(key, part):
    return visit_layout(key)


def draw_piece_patch(key, part):
    base_key = jax.random.fold_in(key, 7202)
    row_total = PIECES // (PIECE_DEV * PATCHES)
    block_total = PIECES // PIECE_DEV
    hot_all = jax.random.randint(jax.random.fold_in(base_key, 1), (row_total,), 0, PATCHES).astype(jnp.int32)

    def one_block(block_id):
        sub_key = jax.random.fold_in(base_key, block_id + 17)
        hot_patch = hot_all[block_id // PATCHES]
        others = jax.random.permutation(jax.random.fold_in(sub_key, 1), PATCHES - 1).astype(jnp.int32)
        others = others + (others >= hot_patch).astype(jnp.int32)
        start_shift = jax.random.randint(jax.random.fold_in(sub_key, 2), (), 0, CAP).astype(jnp.int32)
        rank_list = jnp.arange(PIECE_DEV, dtype=jnp.int32) - CAP
        pick_index = jnp.clip((rank_list + start_shift) // CAP, 0, PATCHES - 2)
        labels = jnp.where(rank_list < 0, hot_patch, others[pick_index])
        shuffle = jax.random.permutation(jax.random.fold_in(sub_key, 3), PIECE_DEV)
        return labels[shuffle].astype(jnp.int32)
    return jax.vmap(one_block)(jnp.arange(block_total, dtype=jnp.int32)).reshape(PIECES).astype(jnp.int32)


def draw_pieces(key, part):
    local_visit = visit_layout(key)
    block_of = jnp.arange(PIECES, dtype=jnp.int32) // PIECE_DEV
    column = (block_of % PATCHES).astype(jnp.float32)
    visit_id = block_of // PATCHES * VIS_DEV + local_visit
    level_key = jax.random.fold_in(key, 7303)
    keys_all = jax.random.split(level_key, 6)
    levels = jax.random.uniform(keys_all[0], (VISITS,), jnp.float32, -2.0, 2.0)
    rise_factor = 1.0 + 2.0 * column / (PATCHES - 1)
    noise_field = jax.random.normal(keys_all[1], (PIECES, PIX, PIX), jnp.float32)
    row_scale = jnp.exp(jax.random.uniform(keys_all[2], (PIECES, PIX), jnp.float32, -0.6931472, 1.6094379))
    amplitude = jax.random.uniform(keys_all[3], (VISITS,), jnp.float32, 0.5, 1.5)
    row_order = jax.random.randint(keys_all[4], (VISITS,), 0, TERMS).astype(jnp.float32)
    col_order = jax.random.randint(keys_all[5], (VISITS,), 0, TERMS).astype(jnp.float32)
    grid_coord = (2.0 * jnp.arange(PIX).astype(jnp.float32) + 1.0) / PIX - 1.0
    angles = jnp.arccos(grid_coord)
    row_wave = jnp.cos(row_order[visit_id][:, None] * angles[None, :])
    col_wave = jnp.cos(col_order[visit_id][:, None] * angles[None, :])
    smooth = levels[visit_id][:, None, None] + amplitude[visit_id][:, None, None] * row_wave[:, :, None] * col_wave[:, None, :]
    return (noise_field * row_scale[:, :, None] + rise_factor[:, None, None] * smooth).astype(jnp.float32)


def plant(array, stream_key, least, largest):
    index_at = [jax.random.randint(jax.random.fold_in(stream_key, axis), (), 0, length) for axis, length in enumerate(array.shape)]
    widest = array.shape.index(max(array.shape))
    neighbour = index_at[:widest] + [(index_at[widest] + 1) % array.shape[widest]] + index_at[widest + 1:]
    return array.at[tuple(index_at)].set(least).at[tuple(neighbour)].set(largest)


def block_levels(stream_key, shape, cuts, least, largest):
    level, own = 1.0, jax.random.fold_in(stream_key, 6)
    for dim, shards_of in cuts:
        heights = jnp.exp(jax.random.uniform(jax.random.fold_in(own, dim), (shards_of,), jnp.float32, least / len(cuts), largest / len(cuts)))
        level = level * jnp.repeat(heights, shape[dim] // shards_of).reshape([-1 if axis == dim else 1 for axis in range(len(shape))])
    return level


def noise(key, dims, spread, limit, cuts=(), kind=jnp.bfloat16):
    level = block_levels(key, dims, cuts, -0.22, 0.18) if cuts else 1.0
    drawn = jax.random.normal(key, dims, jnp.float32) * spread * level
    return jnp.minimum(jnp.maximum(drawn, -limit), limit).astype(kind)


def setup_inputs(seed: int = 0) -> dict:
    key_list = jax.random.split(jax.random.key(seed), 8)
    pieces = draw_pieces(jax.random.fold_in(key_list[7], 71), 0)
    ref_patch = noise(key_list[1], (PATCHES, PIX, PIX), 1.0, 6.0, ((0, 8), (1, 4)), jnp.float32)
    piece_patch = draw_piece_patch(jax.random.fold_in(key_list[7], 71), 0)
    piece_visit = draw_piece_visit(jax.random.fold_in(key_list[7], 71), 0)
    anchors = plant(jax.random.randint(key_list[4], (PIECES, 2), 0, TILE - PIX + 1), jax.random.fold_in(key_list[4], 1), 0, TILE - PIX).astype(jnp.int32)
    shifts = plant(jax.random.randint(key_list[5], (PIECES, 2), -2, 3), jax.random.fold_in(key_list[5], 1), -2, 2).astype(jnp.int32)
    phases = jnp.clip(1.0 * jax.random.uniform(key_list[6], (PIECES, 2), jnp.float32) ** block_levels(key_list[6], (PIECES, 2), ((0, 32),), -0.2, 0.2), 0.0, 1.0)
    return {"pieces": pieces, "ref_patch": ref_patch, "piece_patch": piece_patch, "piece_visit": piece_visit, "anchors": anchors, "shifts": shifts, "phases": phases}


exact_mode = lax.Precision.HIGHEST


def lanczos_matrix(band_shift, sub_phase, side_len):
    positions = jnp.arange(side_len, dtype=jnp.int32)
    offset = (positions[:, None] + band_shift - positions[None, :]).astype(sub_phase.dtype) + sub_phase
    weight = jnp.sinc(offset) * jnp.sinc(offset / 3.0)
    return jnp.where(jnp.abs(offset) < 3.0, weight, jnp.zeros_like(weight))


def chebyshev_rows(first_pixel, side_len):
    pixels = (first_pixel + jnp.arange(side_len, dtype=jnp.int32)).astype(jnp.float32)
    coordinate = (2.0 * pixels + 1.0) / TILE - 1.0
    orders = jnp.arange(TERMS, dtype=jnp.int32).astype(jnp.float32)
    return jnp.cos(orders[:, None] * jnp.arccos(coordinate)[None, :])


def warp_piece(slab_image, row_shift, col_shift, row_phase, col_phase):
    side_len = slab_image.shape[0]
    left_matrix = lanczos_matrix(row_shift, row_phase, side_len)
    right_matrix = lanczos_matrix(col_shift, col_phase, side_len)
    middle = jnp.dot(left_matrix, slab_image, precision=exact_mode)
    return jnp.dot(middle, right_matrix.T, precision=exact_mode)


def reference(pieces, ref_patch, piece_patch, piece_visit, anchors, shifts, phases):
    per_visit = PATCHES * PIECE_DEV // VIS_DEV
    row_of = jnp.arange(PIECES, dtype=jnp.int32) // (PIECE_DEV * PATCHES)
    visit_of = (row_of * VIS_DEV + piece_visit).astype(jnp.int32)

    def difference(inputs):
        slab_image, patch_id, band_pair, phase_pair = inputs
        warped = warp_piece(slab_image, band_pair[0], band_pair[1], phase_pair[0], phase_pair[1])
        return warped - lax.dynamic_index_in_dim(ref_patch, patch_id, 0, keepdims=False)

    diffs = lax.map(difference, (pieces, piece_patch, shifts, phases))

    def project(inputs):
        diff_image, anchor_pair = inputs
        row_basis = chebyshev_rows(anchor_pair[0], PIX)
        col_basis = chebyshev_rows(anchor_pair[1], PIX)
        middle = jnp.dot(row_basis, diff_image, precision=exact_mode)
        return jnp.dot(middle, col_basis.T, precision=exact_mode)

    partial_value = lax.map(project, (diffs, anchors))
    totals = jax.ops.segment_sum(partial_value, visit_of, num_segments=VISITS)
    coefficients = totals / (per_visit * PIX * PIX)

    def subtract_fit(inputs):
        diff_image, anchor_pair, visit_id = inputs
        row_basis = chebyshev_rows(anchor_pair[0], PIX)
        col_basis = chebyshev_rows(anchor_pair[1], PIX)
        chosen = lax.dynamic_index_in_dim(coefficients, visit_id, 0, keepdims=False)
        middle = jnp.dot(row_basis.T, chosen, precision=exact_mode)
        return diff_image - jnp.dot(middle, col_basis, precision=exact_mode)

    matched = lax.map(subtract_fit, (diffs, anchors, visit_of))
    return matched, coefficients
```

```python
import functools
import itertools

import jax
import jax.numpy as jnp
from jax import lax
from jax.experimental import pallas as pl
from jax.experimental.pallas import tpu as pltpu
from jax.sharding import PartitionSpec as P

VIS_DEV = 4
TERMS = 17
TILE = 4096
TAPS = 6
LINE = 4
TROWS = 32
BLOCK = 128
MESH = pl.DeviceIdType.MESH
exact_mode = lax.Precision.HIGHEST
bf16 = jnp.bfloat16
f32 = jnp.float32


def split(x):
    hi = x.astype(bf16)
    return hi, (x - hi.astype(f32)).astype(bf16)


def mm(a, b):
    return jnp.dot(a, b, preferred_element_type=f32)


def tap_weights(phases):
    offset = jnp.arange(-3, TAPS - 3, dtype=jnp.int32).astype(f32)[None, None, :] + phases[:, :, None]
    weight = jnp.sinc(offset) * jnp.sinc(offset / 3.0)
    weight = jnp.where(jnp.abs(offset) < 3.0, weight, jnp.zeros_like(weight))
    return weight.reshape(phases.shape[0], 2 * TAPS)


def fill_basis(anchor_ref, rows, cols, side):
    count = anchor_ref.shape[0]
    pixel = lax.broadcasted_iota(jnp.int32, (count, side), 1)
    for ref, axis in ((rows, 0), (cols, 1)):
        ref[...] = jnp.zeros(ref.shape, f32)
        first = anchor_ref[:, axis : axis + 1]
        u = (2.0 * (first + pixel).astype(f32) + 1.0) / TILE - 1.0
        before, now = jnp.ones_like(u), u
        ref[:, 0, :] = before
        for m in range(1, TERMS):
            ref[:, m, :] = now
            before, now = now, 2.0 * u * now - before


def pick(index, values):
    out = jnp.int32(values[0])
    for place in range(1, len(values)):
        out = jnp.where(index == place, jnp.int32(values[place]), out)
    return out


def nearest(size, rank):
    return [sorted(range(size), key=lambda j: (abs(j - i), j))[rank] for i in range(size)]


class Gather:
    def __init__(self, sizes, parts, rows):
        self.sizes, self.parts, self.rows = sizes, parts, rows
        self.chips = sizes[0] * sizes[1] * sizes[2]
        self.sends = 0
        self.events = []
        offset = 0
        for number, (height, order) in enumerate(parts):
            for ranks in itertools.product(*(range(n) for n in sizes)):
                self.events.append((sum(ranks), number, ranks, offset, height, order))
            offset += height
        self.events.sort(key=lambda e: (e[0], e[1]))
        slots = []
        for _, number, ranks, offset, height, order in self.events:
            stage = max([-1] + [j for j in range(3) if ranks[order[j]]])
            kinds = []
            if stage >= 0 and sizes[order[stage]] > 2:
                kinds.append(("on", order[stage]))
            for axis in order[stage + 1 :]:
                kinds += [("up", axis), ("down", axis)] if sizes[axis] > 2 else [("swap", axis)]
            kinds.append(("core", 0))
            slots.append([(kind, axis, self.sends + j) for j, (kind, axis) in enumerate(kinds)])
            self.sends += len(kinds)
        self.slots = slots

    def bind(self, buffer, send_sem, recv_sem, core_sem):
        sa, sb, sy = self.sizes
        place, visit = lax.axis_index("patch"), lax.axis_index("visit")
        self.me = (place // sb, place % sb, visit // 2)
        self.core = visit % 2
        self.buffer, self.send_sem, self.recv_sem, self.core_sem = buffer, send_sem, recv_sem, core_sem

    def device(self, coords, core):
        return (coords[2] * 2 + core, coords[0] * self.sizes[1] + coords[1])

    def source(self, ranks):
        return [
            self.me[j] if ranks[j] == 0 else pick(self.me[j], nearest(self.sizes[j], ranks[j]))
            for j in range(3)
        ]

    def view(self, at, core, offset, height):
        start = pl.multiple_of((at[2] * 2 + core) * self.rows + offset, 8)
        return self.buffer.at[at[0] * self.sizes[1] + at[1], pl.ds(start, height), :]

    def index(self, number, at):
        return number * self.chips + (at[0] * self.sizes[1] + at[1]) * self.sizes[2] + at[2]

    def copies(self, event):
        _, number, ranks, offset, height, _ = self.events[event]
        at = self.source(ranks)
        view = self.view(at, self.core, offset, height)
        index = self.index(number, at)
        for kind, axis, slot in self.slots[event]:
            to, valid, sem, core = list(self.me), None, self.recv_sem, self.core
            if kind == "core":
                sem, core = self.core_sem, 1 - self.core
            elif kind == "swap":
                to[axis] = 1 - self.me[axis]
            else:
                if kind == "on":
                    step = jnp.where(at[axis] < self.me[axis], 1, -1)
                else:
                    step = 1 if kind == "up" else -1
                to[axis] = self.me[axis] + step
                valid = jnp.logical_and(to[axis] >= 0, to[axis] < self.sizes[axis])
            yield valid, pltpu.make_async_remote_copy(
                src_ref=view,
                dst_ref=view,
                send_sem=self.send_sem.at[slot],
                recv_sem=sem.at[index],
                device_id=self.device(to, core),
                device_id_type=MESH,
            )

    def each(self, event, act):
        for valid, copy in self.copies(event):
            if valid is None:
                act(copy)
            else:
                pl.when(valid)(functools.partial(act, copy))

    def arrive(self, event, core):
        _, number, ranks, offset, height, _ = self.events[event]
        at = self.source(ranks)
        owner = 1 - self.core if core else self.core
        view = self.view(at, owner, offset, height)
        sem = self.core_sem if core else self.recv_sem
        pltpu.make_async_remote_copy(
            src_ref=view,
            dst_ref=view,
            send_sem=self.send_sem.at[0],
            recv_sem=sem.at[self.index(number, at)],
            device_id=self.device(self.me, 1 - self.core),
            device_id_type=MESH,
        ).wait_recv()

    def run(self, event):
        if sum(self.events[event][2]):
            self.arrive(event, False)
        self.each(event, lambda copy: copy.start())

    def finish(self):
        for event in range(len(self.events)):
            self.arrive(event, True)

    def drain(self):
        for event in range(len(self.events)):
            self.each(event, lambda copy: copy.wait_send())


def greet(gather, patch_total):
    barrier = pltpu.get_barrier_semaphore()
    place, visit = lax.axis_index("patch"), lax.axis_index("visit")
    ny = gather.sizes[2]
    y, core = gather.me[2], gather.core

    def call(device):
        pl.semaphore_signal(barrier, inc=1, device_id=device, device_id_type=MESH)

    call((y * 2 + 1 - core, place))
    for step in (1, -1):
        pl.when(jnp.logical_and(y + step >= 0, y + step < ny))(
            lambda step=step: call(((y + step) * 2 + core, place))
        )
    for shift in range(1, patch_total):
        call((visit, (place + shift) % patch_total))
    beside = jnp.where(y > 0, 1, 0) + jnp.where(y < ny - 1, 1, 0)
    pl.semaphore_wait(barrier, patch_total + beside)


def fit_kernel(
    gather,
    patch_total,
    scale,
    pieces,
    ref_patch,
    anchors,
    piece_patch,
    piece_visit,
    shifts,
    weights,
    diff_out,
    coef_out,
    work,
    everyone,
    xhi,
    xlo,
    strip,
    rhi,
    rlo,
    vrow,
    vcol,
    sums,
    gathered,
    in_sem,
    out_sem,
    own_sem,
    send_sem,
    recv_sem,
    core_sem,
    sum_send,
    sum_recv,
):
    count, side = work.shape[0], work.shape[1]
    pad = BLOCK // 2
    place, visit = lax.axis_index("patch"), lax.axis_index("visit")
    gather.bind(everyone, send_sem, recv_sem, core_sem)

    start = pl.multiple_of(visit * gather.rows, 8)
    own = pltpu.make_async_copy(
        ref_patch.at[0], everyone.at[place, pl.ds(start, gather.rows), :], own_sem
    )
    own.start()
    for k in range(count):
        pltpu.make_async_copy(pieces.at[k], work.at[k], in_sem.at[k]).start()
    greet(gather, patch_total)
    own.wait()
    local = [e for e in range(len(gather.events)) if sum(gather.events[e][2]) == 0]
    for event in local:
        gather.run(event)

    fill_basis(anchors, vrow, vcol, side)
    for ref in (xhi, xlo):
        ref[0:pad, :] = jnp.zeros((pad, side), bf16)
        ref[pad + side : 2 * pad + side, :] = jnp.zeros((pad, side), bf16)
    for ref in (rhi, rlo):
        ref[...] = jnp.zeros((side, side), bf16)
    sums[...] = jnp.zeros_like(sums)

    blocks = side // BLOCK
    ticks = count * blocks
    remote = [e for e in range(len(gather.events)) if sum(gather.events[e][2])]

    def banded(k, axis, distance):
        out = jnp.zeros(distance.shape, f32)
        for tap in range(TAPS):
            out = jnp.where(distance == tap - 3, weights[k, axis * TAPS + tap], out)
        return split(out)

    def prepare(k):
        pltpu.make_async_copy(pieces.at[k], work.at[k], in_sem.at[k]).wait()
        for q in range(blocks):
            hi, lo = split(work[k, q * BLOCK : (q + 1) * BLOCK, :])
            xhi[pad + q * BLOCK : pad + (q + 1) * BLOCK, :] = hi
            xlo[pad + q * BLOCK : pad + (q + 1) * BLOCK, :] = lo
        shape = (BLOCK, 2 * BLOCK)
        d = lax.broadcasted_iota(jnp.int32, shape, 0) - lax.broadcasted_iota(jnp.int32, shape, 1)
        hi, lo = banded(k, 0, d + pad + shifts[k, 0])
        strip[0:BLOCK, :] = hi
        strip[BLOCK : 2 * BLOCK, :] = lo
        shape = (BLOCK, BLOCK)
        d = lax.broadcasted_iota(jnp.int32, shape, 1) - lax.broadcasted_iota(jnp.int32, shape, 0)
        for step in (-1, 0, 1):
            hi, lo = banded(k, 1, d + step * BLOCK + shifts[k, 1])
            for i in range(blocks):
                j = i + step
                if 0 <= j < blocks:
                    rhi[i * BLOCK : (i + 1) * BLOCK, j * BLOCK : (j + 1) * BLOCK] = hi
                    rlo[i * BLOCK : (i + 1) * BLOCK, j * BLOCK : (j + 1) * BLOCK] = lo

    @pl.loop(0, ticks)
    def _(t):
        k, q = t // blocks, t % blocks
        pl.when(q == 0)(lambda: prepare(k))
        base = pl.multiple_of(q * BLOCK, BLOCK)
        window = pl.ds(base, 2 * BLOCK)
        both = mm(strip[...], xhi[window, :])
        middle = both[:BLOCK] + both[BLOCK:] + mm(strip[0:BLOCK, :], xlo[window, :])
        hi, lo = split(middle)
        both = mm(jnp.concatenate([hi, lo], 0), rhi[...])
        work[k, pl.ds(base, BLOCK), :] = both[:BLOCK] + both[BLOCK:] + mm(hi, rlo[...])
        for tick in range(ticks):
            due = [e for n, e in enumerate(remote) if (n * ticks) // len(remote) == tick]
            if due:
                pl.when(t == tick)(lambda due=due: [gather.run(e) for e in due] and None)

    gather.finish()

    half = side // 2

    @pl.loop(0, count)
    def _(k):
        patch_id = piece_patch[k]
        hi, lo = split(vrow[k])
        stacked = jnp.concatenate([hi, lo], 0)
        total = jnp.zeros((TROWS, side), f32)
        for h in range(2):
            rows = slice(h * half, (h + 1) * half)
            diff = work[k, rows, :] - everyone[patch_id, rows, :]
            work[k, rows, :] = diff
            dhi, dlo = split(diff)
            both = mm(stacked[:, rows], dhi)
            total = total + both[:TROWS] + both[TROWS:] + mm(hi[:, rows], dlo)
        pltpu.make_async_copy(work.at[k], diff_out.at[k], out_sem.at[k]).start()
        columns = vcol[k]
        spread = jnp.concatenate(
            [jnp.where(piece_visit[k] == v, columns, 0.0) for v in range(VIS_DEV)], 0
        )
        sums[...] += lax.dot_general(
            total, spread, (((1,), (1,)), ((), ())), precision=exact_mode, preferred_element_type=f32
        )

    def exchange(shift):
        return pltpu.make_async_remote_copy(
            src_ref=sums,
            dst_ref=gathered.at[place],
            send_sem=sum_send.at[shift],
            recv_sem=sum_recv.at[place],
            device_id=(visit, (place + shift) % patch_total),
            device_id_type=MESH,
        )

    for shift in range(1, patch_total):
        exchange(shift).start()
    gathered[place] = sums[...]
    gather.drain()
    for shift in range(1, patch_total):
        origin = (place + shift) % patch_total
        pltpu.make_async_remote_copy(
            src_ref=sums,
            dst_ref=gathered.at[origin],
            send_sem=sum_send.at[shift],
            recv_sem=sum_recv.at[origin],
            device_id=(visit, origin),
            device_id_type=MESH,
        ).wait_recv()
    total = gathered[0]
    for origin in range(1, patch_total):
        total = total + gathered[origin]
    coef_out[...] = total / scale
    for shift in range(1, patch_total):
        exchange(shift).wait_send()
    for k in range(count):
        pltpu.make_async_copy(work.at[k], diff_out.at[k], out_sem.at[k]).wait()


def subtract_kernel(piece_visit, diff, coef, anchors, out, vrow, vcol):
    k = pl.program_id(0)
    side = diff.shape[1]
    pl.when(k == 0)(lambda: fill_basis(anchors, vrow, vcol, side))
    chosen = coef[piece_visit[k]]
    inner = jnp.dot(chosen, vcol[k], precision=exact_mode, preferred_element_type=f32)
    ihi, ilo = split(inner)
    rhi, rlo = split(vrow[k])
    fit = lax.dot_general(
        jnp.concatenate([rhi, rhi, rlo], 0),
        jnp.concatenate([ihi, ilo, ihi], 0),
        (((0,), (0,)), ((), ())),
        preferred_element_type=f32,
    )
    out[0] = diff[0] - fit


def body(nv, pieces, ref_patch, piece_patch, piece_visit, anchors, shifts, phases):
    count, side = pieces.shape[0], pieces.shape[1]
    patch_total = lax.axis_size("patch")
    rows = ref_patch.shape[1]
    sizes = (LINE, patch_total // LINE, nv // 2)
    parts = [(rows // 2, (0, 1, 2)), (rows // 2, (0, 2, 1))]
    gather = Gather(sizes, parts, rows)
    weights = tap_weights(phases)
    scale = float(patch_total * (count // VIS_DEV) * side * side)
    anywhere = pl.BlockSpec(memory_space=pl.ANY)
    vmem = pl.BlockSpec(memory_space=pltpu.VMEM)
    smem = pl.BlockSpec(memory_space=pltpu.SMEM)
    lanes = VIS_DEV * TROWS
    dma = pltpu.SemaphoreType.DMA
    diff, sums = pl.pallas_call(
        functools.partial(fit_kernel, gather, patch_total, scale),
        out_shape=(
            jax.ShapeDtypeStruct(pieces.shape, f32),
            jax.ShapeDtypeStruct((TROWS, lanes), f32),
        ),
        in_specs=[anywhere, anywhere, vmem, smem, smem, smem, smem],
        out_specs=(anywhere, vmem),
        scratch_shapes=[
            pltpu.VMEM((count, side, side), f32),
            pltpu.VMEM((patch_total, side, side), f32),
            pltpu.VMEM((side + BLOCK, side), bf16),
            pltpu.VMEM((side + BLOCK, side), bf16),
            pltpu.VMEM((2 * BLOCK, 2 * BLOCK), bf16),
            pltpu.VMEM((side, side), bf16),
            pltpu.VMEM((side, side), bf16),
            pltpu.VMEM((count, TROWS, side), f32),
            pltpu.VMEM((count, TROWS, side), f32),
            pltpu.VMEM((TROWS, lanes), f32),
            pltpu.VMEM((patch_total, TROWS, lanes), f32),
            dma((count,)),
            dma((count,)),
            dma,
            dma((gather.sends,)),
            dma((len(parts) * gather.chips,)),
            dma((len(parts) * gather.chips,)),
            dma((patch_total,)),
            dma((patch_total,)),
        ],
        compiler_params=pltpu.CompilerParams(
            collective_id=0, has_side_effects=True, vmem_limit_bytes=48 * 2**20
        ),
        name="gather_warp_project",
    )(pieces, ref_patch, anchors, piece_patch, piece_visit, shifts, weights)
    table = sums.reshape(TROWS, VIS_DEV, TROWS).transpose(1, 0, 2)
    matched = pl.pallas_call(
        subtract_kernel,
        out_shape=jax.ShapeDtypeStruct(pieces.shape, f32),
        grid=(count,),
        in_specs=[
            smem,
            pl.BlockSpec((1, side, side), lambda k: (k, 0, 0)),
            pl.BlockSpec((VIS_DEV, TROWS, TROWS), lambda k: (0, 0, 0)),
            pl.BlockSpec((count, 2), lambda k: (0, 0)),
        ],
        out_specs=pl.BlockSpec((1, side, side), lambda k: (k, 0, 0)),
        scratch_shapes=[
            pltpu.VMEM((count, TROWS, side), f32),
            pltpu.VMEM((count, TROWS, side), f32),
        ],
        compiler_params=pltpu.CompilerParams(vmem_limit_bytes=32 * 2**20),
        name="subtract_fit",
    )(piece_visit, diff, table, anchors)
    return matched, table[:, :TERMS, :TERMS]


def solution(mesh):
    return jax.shard_map(
        functools.partial(body, mesh.shape["visit"]),
        mesh=mesh,
        in_specs=(
            P(("visit", "patch"), None, None),
            P("patch", "visit", None),
            P(("visit", "patch")),
            P(("visit", "patch")),
            P(("visit", "patch"), None),
            P(("visit", "patch"), None),
            P(("visit", "patch"), None),
        ),
        out_specs=(P(("visit", "patch"), None, None), P("visit", None, None)),
        check_vma=False,
    )
```

```python
import functools
import itertools

import jax
import jax.numpy as jnp
from jax import lax
from jax.experimental import pallas as pl
from jax.experimental.pallas import tpu as pltpu
from jax.sharding import PartitionSpec as P

VIS_DEV = 4
TERMS = 17
TILE = 4096
TAPS = 6
LINE = 4
TROWS = 32
BLOCK = 128
PARTS = ((4, (0, 1, 2)), (4, (0, 2, 1)))
MESH = pl.DeviceIdType.MESH
exact_mode = lax.Precision.HIGHEST
bf16 = jnp.bfloat16
f32 = jnp.float32


def split(x):
    hi = x.astype(bf16)
    return hi, (x - hi.astype(f32)).astype(bf16)


def mm(a, b):
    return jnp.dot(a, b, preferred_element_type=f32)


def tap_weights(phases):
    offset = jnp.arange(-3, TAPS - 3, dtype=jnp.int32).astype(f32)[None, :, None] + phases.T[:, None, :]
    weight = jnp.sinc(offset) * jnp.sinc(offset / 3.0)
    weight = jnp.where(jnp.abs(offset) < 3.0, weight, jnp.zeros_like(weight))
    return weight.reshape(2 * TAPS, phases.shape[0])


def fill_basis(anchor_ref, rows, cols, side):
    count = anchor_ref.shape[1]
    piece = lax.broadcasted_iota(jnp.int32, (count, side), 0)
    pixel = lax.broadcasted_iota(jnp.int32, (count, side), 1)
    for ref, axis in ((rows, 0), (cols, 1)):
        ref[...] = jnp.zeros(ref.shape, f32)
        first = jnp.zeros((count, side), jnp.int32)
        for k in range(count):
            first = jnp.where(piece == k, anchor_ref[axis, k], first)
        u = (2.0 * (first + pixel).astype(f32) + 1.0) / TILE - 1.0
        before, now = jnp.ones_like(u), u
        ref[:, 0, :] = before
        for m in range(1, TERMS):
            ref[:, m, :] = now
            before, now = now, 2.0 * u * now - before


def pick(index, values):
    out = jnp.int32(values[0])
    for place in range(1, len(values)):
        out = jnp.where(index == place, jnp.int32(values[place]), out)
    return out


def nearest(size, rank):
    return [sorted(range(size), key=lambda j: (abs(j - i), j))[rank] for i in range(size)]


class Gather:
    def __init__(self, sizes, parts, rows):
        self.sizes, self.parts, self.rows = sizes, parts, rows
        self.chips = sizes[0] * sizes[1] * sizes[2]
        self.sends = 0
        self.events = []
        offset = 0
        for number, (height, order) in enumerate(parts):
            for ranks in itertools.product(*(range(n) for n in sizes)):
                self.events.append((sum(ranks), number, ranks, offset, height, order))
            offset += height
        self.events.sort(key=lambda e: (e[0], e[1]))
        slots = []
        for _, number, ranks, offset, height, order in self.events:
            stage = max([-1] + [j for j in range(3) if ranks[order[j]]])
            kinds = []
            if stage >= 0 and sizes[order[stage]] > 2:
                kinds.append(("on", order[stage]))
            for axis in order[stage + 1 :]:
                kinds += [("up", axis), ("down", axis)] if sizes[axis] > 2 else [("swap", axis)]
            kinds.append(("core", 0))
            slots.append([(kind, axis, self.sends + j) for j, (kind, axis) in enumerate(kinds)])
            self.sends += len(kinds)
        self.slots = slots

    def bind(self, buffer, send_sem, recv_sem, core_sem):
        sa, sb, sy = self.sizes
        place, visit = lax.axis_index("patch"), lax.axis_index("visit")
        self.me = (place // sb, place % sb, visit // 2)
        self.core = visit % 2
        self.buffer, self.send_sem, self.recv_sem, self.core_sem = buffer, send_sem, recv_sem, core_sem

    def device(self, coords, core):
        return (coords[2] * 2 + core, coords[0] * self.sizes[1] + coords[1])

    def source(self, ranks):
        return [
            self.me[j] if ranks[j] == 0 else pick(self.me[j], nearest(self.sizes[j], ranks[j]))
            for j in range(3)
        ]

    def view(self, at, core, offset, height):
        start = pl.multiple_of((at[2] * 2 + core) * self.rows + offset, 8)
        return self.buffer.at[at[0] * self.sizes[1] + at[1], pl.ds(start, height), :]

    def index(self, number, at):
        return number * self.chips + (at[0] * self.sizes[1] + at[1]) * self.sizes[2] + at[2]

    def copies(self, event):
        _, number, ranks, offset, height, _ = self.events[event]
        at = self.source(ranks)
        view = self.view(at, self.core, offset, height)
        index = self.index(number, at)
        for kind, axis, slot in self.slots[event]:
            to, valid, sem, core = list(self.me), None, self.recv_sem, self.core
            if kind == "core":
                sem, core = self.core_sem, 1 - self.core
            elif kind == "swap":
                to[axis] = 1 - self.me[axis]
            else:
                if kind == "on":
                    step = jnp.where(at[axis] < self.me[axis], 1, -1)
                else:
                    step = 1 if kind == "up" else -1
                to[axis] = self.me[axis] + step
                valid = jnp.logical_and(to[axis] >= 0, to[axis] < self.sizes[axis])
            yield valid, pltpu.make_async_remote_copy(
                src_ref=view,
                dst_ref=view,
                send_sem=self.send_sem.at[slot],
                recv_sem=sem.at[index],
                device_id=self.device(to, core),
                device_id_type=MESH,
            )

    def each(self, event, act):
        for valid, copy in self.copies(event):
            if valid is None:
                act(copy)
            else:
                pl.when(valid)(functools.partial(act, copy))

    def arrive(self, event, core):
        _, number, ranks, offset, height, _ = self.events[event]
        at = self.source(ranks)
        owner = 1 - self.core if core else self.core
        view = self.view(at, owner, offset, height)
        sem = self.core_sem if core else self.recv_sem
        pltpu.make_async_remote_copy(
            src_ref=view,
            dst_ref=view,
            send_sem=self.send_sem.at[0],
            recv_sem=sem.at[self.index(number, at)],
            device_id=self.device(self.me, 1 - self.core),
            device_id_type=MESH,
        ).wait_recv()

    def run(self, event):
        if sum(self.events[event][2]):
            self.arrive(event, False)
        self.each(event, lambda copy: copy.start())

    def finish(self):
        for event in range(len(self.events)):
            self.arrive(event, True)

    def drain(self):
        for event in range(len(self.events)):
            self.each(event, lambda copy: copy.wait_send())


def greet(gather, patch_total):
    barrier = pltpu.get_barrier_semaphore()
    place, visit = lax.axis_index("patch"), lax.axis_index("visit")
    ny = gather.sizes[2]
    y, core = gather.me[2], gather.core

    def call(device):
        pl.semaphore_signal(barrier, inc=1, device_id=device, device_id_type=MESH)

    call((y * 2 + 1 - core, place))
    for step in (1, -1):
        pl.when(jnp.logical_and(y + step >= 0, y + step < ny))(
            lambda step=step: call(((y + step) * 2 + core, place))
        )
    for shift in range(1, patch_total):
        call((visit, (place + shift) % patch_total))
    beside = jnp.where(y > 0, 1, 0) + jnp.where(y < ny - 1, 1, 0)
    pl.semaphore_wait(barrier, patch_total + beside)


def fit_kernel(
    gather,
    patch_total,
    scale,
    pieces,
    ref_patch,
    anchors,
    piece_patch,
    piece_visit,
    shifts,
    weights,
    diff_out,
    coef_out,
    left_out,
    vcol_out,
    work,
    everyone,
    xhi,
    xlo,
    strip,
    rhi,
    rlo,
    vrow,
    vcol,
    left,
    chi,
    clo,
    sums,
    gathered,
    in_sem,
    out_sem,
    basis_sem,
    own_sem,
    send_sem,
    recv_sem,
    core_sem,
    sum_send,
    sum_recv,
):
    count, side = work.shape[0], work.shape[1]
    pad = BLOCK // 2
    place, visit = lax.axis_index("patch"), lax.axis_index("visit")
    gather.bind(everyone, send_sem, recv_sem, core_sem)

    start = pl.multiple_of(visit * gather.rows, 8)
    own = pltpu.make_async_copy(
        ref_patch.at[0], everyone.at[place, pl.ds(start, gather.rows), :], own_sem
    )
    own.start()
    for k in range(count):
        pltpu.make_async_copy(pieces.at[k], work.at[k], in_sem.at[k]).start()
    greet(gather, patch_total)
    own.wait()
    local = [e for e in range(len(gather.events)) if sum(gather.events[e][2]) == 0]
    for event in local:
        gather.run(event)

    fill_basis(anchors, vrow, vcol, side)

    @pl.loop(0, count)
    def _(k):
        hi, lo = split(vrow[k])
        hi = hi.astype(f32)
        stack = jnp.concatenate([hi, hi, lo.astype(f32), jnp.zeros_like(hi)], 0)
        left[k] = stack.T.astype(bf16)
        columns = vcol[k]
        spread = jnp.concatenate(
            [jnp.where(piece_visit[k] == v, columns, 0.0) for v in range(VIS_DEV)], 0
        )
        hi, lo = split(spread)
        chi[k] = hi.astype(f32).T.astype(bf16)
        clo[k] = lo.astype(f32).T.astype(bf16)

    basis = [
        pltpu.make_async_copy(left, left_out, basis_sem.at[0]),
        pltpu.make_async_copy(vcol, vcol_out, basis_sem.at[1]),
    ]
    for copy in basis:
        copy.start()
    for ref in (xhi, xlo):
        ref[0:pad, :] = jnp.zeros((pad, side), bf16)
        ref[pad + side : 2 * pad + side, :] = jnp.zeros((pad, side), bf16)
    for ref in (rhi, rlo):
        ref[...] = jnp.zeros((side, side), bf16)
    sums[...] = jnp.zeros_like(sums)

    blocks = side // BLOCK
    ticks = count * blocks
    remote = [e for e in range(len(gather.events)) if sum(gather.events[e][2])]

    def banded(k, axis, distance):
        out = jnp.zeros(distance.shape, f32)
        for tap in range(TAPS):
            out = jnp.where(distance == tap - 3, weights[axis * TAPS + tap, k], out)
        return split(out)

    def prepare(k):
        pltpu.make_async_copy(pieces.at[k], work.at[k], in_sem.at[k]).wait()
        for q in range(blocks):
            hi, lo = split(work[k, q * BLOCK : (q + 1) * BLOCK, :])
            xhi[pad + q * BLOCK : pad + (q + 1) * BLOCK, :] = hi
            xlo[pad + q * BLOCK : pad + (q + 1) * BLOCK, :] = lo
        shape = (BLOCK, 2 * BLOCK)
        d = lax.broadcasted_iota(jnp.int32, shape, 0) - lax.broadcasted_iota(jnp.int32, shape, 1)
        hi, lo = banded(k, 0, d + pad + shifts[0, k])
        strip[0:BLOCK, :] = hi
        strip[BLOCK : 2 * BLOCK, :] = lo
        shape = (BLOCK, BLOCK)
        d = lax.broadcasted_iota(jnp.int32, shape, 1) - lax.broadcasted_iota(jnp.int32, shape, 0)
        for step in (-1, 0, 1):
            hi, lo = banded(k, 1, d + step * BLOCK + shifts[1, k])
            for i in range(blocks):
                j = i + step
                if 0 <= j < blocks:
                    rhi[i * BLOCK : (i + 1) * BLOCK, j * BLOCK : (j + 1) * BLOCK] = hi
                    rlo[i * BLOCK : (i + 1) * BLOCK, j * BLOCK : (j + 1) * BLOCK] = lo

    @pl.loop(0, ticks)
    def _(t):
        k, q = t // blocks, t % blocks
        pl.when(q == 0)(lambda: prepare(k))
        base = pl.multiple_of(q * BLOCK, BLOCK)
        window = pl.ds(base, 2 * BLOCK)
        both = mm(strip[...], xhi[window, :])
        middle = both[:BLOCK] + both[BLOCK:] + mm(strip[0:BLOCK, :], xlo[window, :])
        hi, lo = split(middle)
        both = mm(jnp.concatenate([hi, lo], 0), rhi[...])
        work[k, pl.ds(base, BLOCK), :] = both[:BLOCK] + both[BLOCK:] + mm(hi, rlo[...])
        for tick in range(ticks):
            due = [e for n, e in enumerate(remote) if ticks // 7 + (n * (ticks - ticks // 7)) // len(remote) == tick]
            if due:
                pl.when(t == tick)(lambda due=due: [gather.run(e) for e in due] and None)

    gather.finish()

    half = side // 2

    @pl.loop(0, count)
    def _(k):
        patch_id = piece_patch[k]
        hi, lo = split(vrow[k])
        stacked = jnp.concatenate([hi, lo], 0)
        total = jnp.zeros((TROWS, side), f32)
        for h in range(2):
            rows = slice(h * half, (h + 1) * half)
            diff = work[k, rows, :] - everyone[patch_id, rows, :]
            work[k, rows, :] = diff
            dhi, dlo = split(diff)
            both = mm(stacked[:, rows], dhi)
            total = total + both[:TROWS] + both[TROWS:] + mm(hi[:, rows], dlo)
        pltpu.make_async_copy(work.at[k], diff_out.at[k], out_sem.at[k]).start()
        thi, tlo = split(total)
        both = mm(jnp.concatenate([thi, tlo], 0), chi[k])
        sums[...] += both[:TROWS] + both[TROWS:] + mm(thi, clo[k])

    def exchange(shift):
        return pltpu.make_async_remote_copy(
            src_ref=sums,
            dst_ref=gathered.at[place],
            send_sem=sum_send.at[shift],
            recv_sem=sum_recv.at[place],
            device_id=(visit, (place + shift) % patch_total),
            device_id_type=MESH,
        )

    for shift in range(1, patch_total):
        exchange(shift).start()
    gathered[place] = sums[...]
    gather.drain()
    for shift in range(1, patch_total):
        origin = (place + shift) % patch_total
        pltpu.make_async_remote_copy(
            src_ref=sums,
            dst_ref=gathered.at[origin],
            send_sem=sum_send.at[shift],
            recv_sem=sum_recv.at[origin],
            device_id=(visit, origin),
            device_id_type=MESH,
        ).wait_recv()
    total = gathered[0]
    for origin in range(1, patch_total):
        total = total + gathered[origin]
    total = total / scale
    for v in range(VIS_DEV):
        coef_out[v] = total[:, v * TROWS : (v + 1) * TROWS]
    for copy in basis:
        copy.wait()
    for shift in range(1, patch_total):
        exchange(shift).wait_send()
    for k in range(count):
        pltpu.make_async_copy(work.at[k], diff_out.at[k], out_sem.at[k]).wait()


def subtract_kernel(piece_visit, diff, coef, left, vcol, out, right):
    k = pl.program_id(0)
    count = piece_visit.shape[0]

    def prepare(j, slot):
        inner = jnp.dot(
            coef[piece_visit[j]], vcol[j], precision=exact_mode, preferred_element_type=f32
        )
        hi, lo = split(inner)
        right[slot] = jnp.concatenate([hi, lo, hi, jnp.zeros_like(hi)], 0)

    pl.when(k == 0)(lambda: prepare(0, 0))
    out[0] = diff[0] - mm(left[0], right[k % 2])
    prepare(jnp.minimum(k + 1, count - 1), (k + 1) % 2)


def body(nv, pieces, ref_patch, piece_patch, piece_visit, anchors, shifts, phases):
    count, side = pieces.shape[0], pieces.shape[1]
    patch_total = lax.axis_size("patch")
    rows = ref_patch.shape[1]
    sizes = (LINE, patch_total // LINE, nv // 2)
    parts = [(rows * eighths // 8, order) for eighths, order in PARTS]
    gather = Gather(sizes, parts, rows)
    weights = tap_weights(phases)
    scale = float(patch_total * (count // VIS_DEV) * side * side)
    anywhere = pl.BlockSpec(memory_space=pl.ANY)
    vmem = pl.BlockSpec(memory_space=pltpu.VMEM)
    smem = pl.BlockSpec(memory_space=pltpu.SMEM)
    lanes = VIS_DEV * TROWS
    dma = pltpu.SemaphoreType.DMA
    diff, table, left, vcol = pl.pallas_call(
        functools.partial(fit_kernel, gather, patch_total, scale),
        out_shape=(
            jax.ShapeDtypeStruct(pieces.shape, f32),
            jax.ShapeDtypeStruct((VIS_DEV, TROWS, TROWS), f32),
            jax.ShapeDtypeStruct((count, side, 4 * TROWS), bf16),
            jax.ShapeDtypeStruct((count, TROWS, side), f32),
        ),
        in_specs=[anywhere, anywhere, smem, smem, smem, smem, smem],
        out_specs=(anywhere, vmem, anywhere, anywhere),
        scratch_shapes=[
            pltpu.VMEM((count, side, side), f32),
            pltpu.VMEM((patch_total, side, side), f32),
            pltpu.VMEM((side + BLOCK, side), bf16),
            pltpu.VMEM((side + BLOCK, side), bf16),
            pltpu.VMEM((2 * BLOCK, 2 * BLOCK), bf16),
            pltpu.VMEM((side, side), bf16),
            pltpu.VMEM((side, side), bf16),
            pltpu.VMEM((count, TROWS, side), f32),
            pltpu.VMEM((count, TROWS, side), f32),
            pltpu.VMEM((count, side, 4 * TROWS), bf16),
            pltpu.VMEM((count, side, lanes), bf16),
            pltpu.VMEM((count, side, lanes), bf16),
            pltpu.VMEM((TROWS, lanes), f32),
            pltpu.VMEM((patch_total, TROWS, lanes), f32),
            dma((count,)),
            dma((count,)),
            dma((2,)),
            dma,
            dma((gather.sends,)),
            dma((len(parts) * gather.chips,)),
            dma((len(parts) * gather.chips,)),
            dma((patch_total,)),
            dma((patch_total,)),
        ],
        compiler_params=pltpu.CompilerParams(
            collective_id=0, has_side_effects=True, vmem_limit_bytes=60 * 2**20
        ),
        name="gather_warp_project",
    )(pieces, ref_patch, anchors.T, piece_patch, piece_visit, shifts.T, weights)
    matched = pl.pallas_call(
        subtract_kernel,
        out_shape=jax.ShapeDtypeStruct(pieces.shape, f32),
        grid=(count,),
        in_specs=[
            smem,
            pl.BlockSpec((1, side, side), lambda k: (k, 0, 0)),
            pl.BlockSpec((VIS_DEV, TROWS, TROWS), lambda k: (0, 0, 0)),
            pl.BlockSpec((1, side, 4 * TROWS), lambda k: (k, 0, 0)),
            pl.BlockSpec((count, TROWS, side), lambda k: (0, 0, 0)),
        ],
        out_specs=pl.BlockSpec((1, side, side), lambda k: (k, 0, 0)),
        scratch_shapes=[pltpu.VMEM((2, 4 * TROWS, side), bf16)],
        compiler_params=pltpu.CompilerParams(vmem_limit_bytes=60 * 2**20),
        name="subtract_fit",
    )(piece_visit, diff, table, left, vcol)
    return matched, table[:, :TERMS, :TERMS]


def solution(mesh):
    return jax.shard_map(
        functools.partial(body, mesh.shape["visit"]),
        mesh=mesh,
        in_specs=(
            P(("visit", "patch"), None, None),
            P("patch", "visit", None),
            P(("visit", "patch")),
            P(("visit", "patch")),
            P(("visit", "patch"), None),
            P(("visit", "patch"), None),
            P(("visit", "patch"), None),
        ),
        out_specs=(P(("visit", "patch"), None, None), P("visit", None, None)),
        check_vma=False,
    )
```

```python
import functools
import itertools

import jax
import jax.numpy as jnp
from jax import lax
from jax.experimental import pallas as pl
from jax.experimental.pallas import tpu as pltpu
from jax.sharding import PartitionSpec as P

VIS_DEV = 4
TERMS = 17
TILE = 4096
TAPS = 6
LINE = 4
TROWS = 32
BLOCK = 128
PARTS = ((4, (0, 1, 2)), (4, (0, 2, 1)))
MESH = pl.DeviceIdType.MESH
exact_mode = lax.Precision.HIGHEST
bf16 = jnp.bfloat16
f32 = jnp.float32


def split(x):
    hi = x.astype(bf16)
    return hi, (x - hi.astype(f32)).astype(bf16)


def mm(a, b):
    return jnp.dot(a, b, preferred_element_type=f32)


def tap_weights(phases):
    offset = jnp.arange(-3, TAPS - 3, dtype=jnp.int32).astype(f32)[None, :, None] + phases.T[:, None, :]
    weight = jnp.sinc(offset) * jnp.sinc(offset / 3.0)
    weight = jnp.where(jnp.abs(offset) < 3.0, weight, jnp.zeros_like(weight))
    return weight.reshape(2 * TAPS, phases.shape[0])


def fill_basis(anchor_ref, rows, cols, side):
    count = anchor_ref.shape[1]
    piece = lax.broadcasted_iota(jnp.int32, (count, side), 0)
    pixel = lax.broadcasted_iota(jnp.int32, (count, side), 1)
    for ref, axis in ((rows, 0), (cols, 1)):
        ref[...] = jnp.zeros(ref.shape, f32)
        first = jnp.zeros((count, side), jnp.int32)
        for k in range(count):
            first = jnp.where(piece == k, anchor_ref[axis, k], first)
        u = (2.0 * (first + pixel).astype(f32) + 1.0) / TILE - 1.0
        before, now = jnp.ones_like(u), u
        ref[:, 0, :] = before
        for m in range(1, TERMS):
            ref[:, m, :] = now
            before, now = now, 2.0 * u * now - before


def pick(index, values):
    out = jnp.int32(values[0])
    for place in range(1, len(values)):
        out = jnp.where(index == place, jnp.int32(values[place]), out)
    return out


def nearest(size, rank):
    return [sorted(range(size), key=lambda j: (abs(j - i), j))[rank] for i in range(size)]


class Gather:
    def __init__(self, sizes, parts, rows):
        self.sizes, self.parts, self.rows = sizes, parts, rows
        self.chips = sizes[0] * sizes[1] * sizes[2]
        self.sends = 0
        self.events = []
        offset = 0
        for number, (height, order) in enumerate(parts):
            for ranks in itertools.product(*(range(n) for n in sizes)):
                self.events.append((sum(ranks), number, ranks, offset, height, order))
            offset += height
        self.events.sort(key=lambda e: (e[0], -e[2][0], e[1]))
        slots = []
        for _, number, ranks, offset, height, order in self.events:
            stage = max([-1] + [j for j in range(3) if ranks[order[j]]])
            kinds = []
            if stage >= 0 and sizes[order[stage]] > 2:
                kinds.append(("on", order[stage]))
            for axis in order[stage + 1 :]:
                kinds += [("up", axis), ("down", axis)] if sizes[axis] > 2 else [("swap", axis)]
            kinds.append(("core", 0))
            slots.append([(kind, axis, self.sends + j) for j, (kind, axis) in enumerate(kinds)])
            self.sends += len(kinds)
        self.slots = slots

    def bind(self, buffer, send_sem, recv_sem, core_sem):
        sa, sb, sy = self.sizes
        place, visit = lax.axis_index("patch"), lax.axis_index("visit")
        self.me = (place // sb, place % sb, visit // 2)
        self.core = visit % 2
        self.buffer, self.send_sem, self.recv_sem, self.core_sem = buffer, send_sem, recv_sem, core_sem

    def device(self, coords, core):
        return (coords[2] * 2 + core, coords[0] * self.sizes[1] + coords[1])

    def source(self, ranks):
        return [
            self.me[j] if ranks[j] == 0 else pick(self.me[j], nearest(self.sizes[j], ranks[j]))
            for j in range(3)
        ]

    def view(self, at, core, offset, height):
        start = pl.multiple_of((at[2] * 2 + core) * self.rows + offset, 8)
        return self.buffer.at[at[0] * self.sizes[1] + at[1], pl.ds(start, height), :]

    def index(self, number, at):
        return number * self.chips + (at[0] * self.sizes[1] + at[1]) * self.sizes[2] + at[2]

    def copies(self, event):
        _, number, ranks, offset, height, _ = self.events[event]
        at = self.source(ranks)
        view = self.view(at, self.core, offset, height)
        index = self.index(number, at)
        for kind, axis, slot in self.slots[event]:
            to, valid, sem, core = list(self.me), None, self.recv_sem, self.core
            if kind == "core":
                sem, core = self.core_sem, 1 - self.core
            elif kind == "swap":
                to[axis] = 1 - self.me[axis]
            else:
                if kind == "on":
                    step = jnp.where(at[axis] < self.me[axis], 1, -1)
                else:
                    step = 1 if kind == "up" else -1
                to[axis] = self.me[axis] + step
                valid = jnp.logical_and(to[axis] >= 0, to[axis] < self.sizes[axis])
            yield valid, pltpu.make_async_remote_copy(
                src_ref=view,
                dst_ref=view,
                send_sem=self.send_sem.at[slot],
                recv_sem=sem.at[index],
                device_id=self.device(to, core),
                device_id_type=MESH,
            )

    def each(self, event, act):
        for valid, copy in self.copies(event):
            if valid is None:
                act(copy)
            else:
                pl.when(valid)(functools.partial(act, copy))

    def arrive(self, event, core):
        _, number, ranks, offset, height, _ = self.events[event]
        at = self.source(ranks)
        owner = 1 - self.core if core else self.core
        view = self.view(at, owner, offset, height)
        sem = self.core_sem if core else self.recv_sem
        pltpu.make_async_remote_copy(
            src_ref=view,
            dst_ref=view,
            send_sem=self.send_sem.at[0],
            recv_sem=sem.at[self.index(number, at)],
            device_id=self.device(self.me, 1 - self.core),
            device_id_type=MESH,
        ).wait_recv()

    def run(self, event):
        if sum(self.events[event][2]):
            self.arrive(event, False)
        self.each(event, lambda copy: copy.start())

    def finish(self):
        for event in range(len(self.events)):
            self.arrive(event, True)

    def drain(self):
        for event in range(len(self.events)):
            self.each(event, lambda copy: copy.wait_send())


def greet(gather, patch_total):
    barrier = pltpu.get_barrier_semaphore()
    place, visit = lax.axis_index("patch"), lax.axis_index("visit")
    ny = gather.sizes[2]
    y, core = gather.me[2], gather.core

    def call(device):
        pl.semaphore_signal(barrier, inc=1, device_id=device, device_id_type=MESH)

    call((y * 2 + 1 - core, place))
    for step in (1, -1):
        pl.when(jnp.logical_and(y + step >= 0, y + step < ny))(
            lambda step=step: call(((y + step) * 2 + core, place))
        )
    for shift in range(1, patch_total):
        call((visit, (place + shift) % patch_total))
    beside = jnp.where(y > 0, 1, 0) + jnp.where(y < ny - 1, 1, 0)
    pl.semaphore_wait(barrier, patch_total + beside)


def fit_kernel(
    gather,
    patch_total,
    scale,
    pieces,
    ref_patch,
    anchors,
    piece_patch,
    piece_visit,
    shifts,
    weights,
    diff_out,
    coef_out,
    left_out,
    vcol_out,
    work,
    everyone,
    xhi,
    xlo,
    strip,
    rhi,
    rlo,
    vrow,
    vcol,
    left,
    chi,
    clo,
    sums,
    gathered,
    in_sem,
    out_sem,
    basis_sem,
    own_sem,
    send_sem,
    recv_sem,
    core_sem,
    sum_send,
    sum_recv,
):
    count, side = work.shape[0], work.shape[1]
    pad = BLOCK // 2
    place, visit = lax.axis_index("patch"), lax.axis_index("visit")
    gather.bind(everyone, send_sem, recv_sem, core_sem)

    start = pl.multiple_of(visit * gather.rows, 8)
    own = pltpu.make_async_copy(
        ref_patch.at[0], everyone.at[place, pl.ds(start, gather.rows), :], own_sem
    )
    own.start()
    for k in range(count):
        pltpu.make_async_copy(pieces.at[k], work.at[k], in_sem.at[k]).start()
    greet(gather, patch_total)
    own.wait()
    local = [e for e in range(len(gather.events)) if sum(gather.events[e][2]) == 0]
    for event in local:
        gather.run(event)

    fill_basis(anchors, vrow, vcol, side)

    @pl.loop(0, count)
    def _(k):
        hi, lo = split(vrow[k])
        hi = hi.astype(f32)
        stack = jnp.concatenate([hi, hi, lo.astype(f32), jnp.zeros_like(hi)], 0)
        left[k] = stack.T.astype(bf16)
        columns = vcol[k]
        spread = jnp.concatenate(
            [jnp.where(piece_visit[k] == v, columns, 0.0) for v in range(VIS_DEV)], 0
        )
        hi, lo = split(spread)
        chi[k] = hi.astype(f32).T.astype(bf16)
        clo[k] = lo.astype(f32).T.astype(bf16)

    basis = [
        pltpu.make_async_copy(left, left_out, basis_sem.at[0]),
        pltpu.make_async_copy(vcol, vcol_out, basis_sem.at[1]),
    ]
    for copy in basis:
        copy.start()
    for ref in (xhi, xlo):
        ref[0:pad, :] = jnp.zeros((pad, side), bf16)
        ref[pad + side : 2 * pad + side, :] = jnp.zeros((pad, side), bf16)
    for ref in (rhi, rlo):
        ref[...] = jnp.zeros((side, side), bf16)
    sums[...] = jnp.zeros_like(sums)

    blocks = side // BLOCK
    ticks = count * blocks
    remote = [e for e in range(len(gather.events)) if sum(gather.events[e][2])]

    def banded(k, axis, distance):
        out = jnp.zeros(distance.shape, f32)
        for tap in range(TAPS):
            out = jnp.where(distance == tap - 3, weights[axis * TAPS + tap, k], out)
        return split(out)

    def prepare(k):
        pltpu.make_async_copy(pieces.at[k], work.at[k], in_sem.at[k]).wait()
        for q in range(blocks):
            hi, lo = split(work[k, q * BLOCK : (q + 1) * BLOCK, :])
            xhi[pad + q * BLOCK : pad + (q + 1) * BLOCK, :] = hi
            xlo[pad + q * BLOCK : pad + (q + 1) * BLOCK, :] = lo
        shape = (BLOCK, 2 * BLOCK)
        d = lax.broadcasted_iota(jnp.int32, shape, 0) - lax.broadcasted_iota(jnp.int32, shape, 1)
        hi, lo = banded(k, 0, d + pad + shifts[0, k])
        strip[0:BLOCK, :] = hi
        strip[BLOCK : 2 * BLOCK, :] = lo
        shape = (BLOCK, BLOCK)
        d = lax.broadcasted_iota(jnp.int32, shape, 1) - lax.broadcasted_iota(jnp.int32, shape, 0)
        for step in (-1, 0, 1):
            hi, lo = banded(k, 1, d + step * BLOCK + shifts[1, k])
            for i in range(blocks):
                j = i + step
                if 0 <= j < blocks:
                    rhi[i * BLOCK : (i + 1) * BLOCK, j * BLOCK : (j + 1) * BLOCK] = hi
                    rlo[i * BLOCK : (i + 1) * BLOCK, j * BLOCK : (j + 1) * BLOCK] = lo

    @pl.loop(0, ticks)
    def _(t):
        k, q = t // blocks, t % blocks
        pl.when(q == 0)(lambda: prepare(k))
        base = pl.multiple_of(q * BLOCK, BLOCK)
        window = pl.ds(base, 2 * BLOCK)
        both = mm(strip[...], xhi[window, :])
        middle = both[:BLOCK] + both[BLOCK:] + mm(strip[0:BLOCK, :], xlo[window, :])
        hi, lo = split(middle)
        both = mm(jnp.concatenate([hi, lo], 0), rhi[...])
        work[k, pl.ds(base, BLOCK), :] = both[:BLOCK] + both[BLOCK:] + mm(hi, rlo[...])
        for tick in range(ticks):
            due = [e for n, e in enumerate(remote) if ticks // 7 + (n * (ticks - ticks // 7)) // len(remote) == tick]
            if due:
                pl.when(t == tick)(lambda due=due: [gather.run(e) for e in due] and None)

    gather.finish()

    half = side // 2

    @pl.loop(0, count)
    def _(k):
        patch_id = piece_patch[k]
        hi, lo = split(vrow[k])
        stacked = jnp.concatenate([hi, lo], 0)
        total = jnp.zeros((TROWS, side), f32)
        for h in range(2):
            rows = slice(h * half, (h + 1) * half)
            diff = work[k, rows, :] - everyone[patch_id, rows, :]
            work[k, rows, :] = diff
            dhi, dlo = split(diff)
            both = mm(stacked[:, rows], dhi)
            total = total + both[:TROWS] + both[TROWS:] + mm(hi[:, rows], dlo)
        pltpu.make_async_copy(work.at[k], diff_out.at[k], out_sem.at[k]).start()
        thi, tlo = split(total)
        both = mm(jnp.concatenate([thi, tlo], 0), chi[k])
        sums[...] += both[:TROWS] + both[TROWS:] + mm(thi, clo[k])

    def exchange(shift):
        return pltpu.make_async_remote_copy(
            src_ref=sums,
            dst_ref=gathered.at[place],
            send_sem=sum_send.at[shift],
            recv_sem=sum_recv.at[place],
            device_id=(visit, (place + shift) % patch_total),
            device_id_type=MESH,
        )

    for shift in range(1, patch_total):
        exchange(shift).start()
    gathered[place] = sums[...]
    gather.drain()
    for shift in range(1, patch_total):
        origin = (place + shift) % patch_total
        pltpu.make_async_remote_copy(
            src_ref=sums,
            dst_ref=gathered.at[origin],
            send_sem=sum_send.at[shift],
            recv_sem=sum_recv.at[origin],
            device_id=(visit, origin),
            device_id_type=MESH,
        ).wait_recv()
    total = gathered[0]
    for origin in range(1, patch_total):
        total = total + gathered[origin]
    total = total / scale
    for v in range(VIS_DEV):
        coef_out[v] = total[:, v * TROWS : (v + 1) * TROWS]
    for copy in basis:
        copy.wait()
    for shift in range(1, patch_total):
        exchange(shift).wait_send()
    for k in range(count):
        pltpu.make_async_copy(work.at[k], diff_out.at[k], out_sem.at[k]).wait()


def subtract_kernel(piece_visit, diff, coef, left, vcol, out, right):
    k = pl.program_id(0)
    count = piece_visit.shape[0]

    def prepare(j, slot):
        inner = jnp.dot(
            coef[piece_visit[j]], vcol[j], precision=exact_mode, preferred_element_type=f32
        )
        hi, lo = split(inner)
        right[slot] = jnp.concatenate([hi, lo, hi, jnp.zeros_like(hi)], 0)

    pl.when(k == 0)(lambda: prepare(0, 0))
    out[0] = diff[0] - mm(left[0], right[k % 2])
    prepare(jnp.minimum(k + 1, count - 1), (k + 1) % 2)


def body(nv, pieces, ref_patch, piece_patch, piece_visit, anchors, shifts, phases):
    count, side = pieces.shape[0], pieces.shape[1]
    patch_total = lax.axis_size("patch")
    rows = ref_patch.shape[1]
    sizes = (LINE, patch_total // LINE, nv // 2)
    parts = [(rows * eighths // 8, order) for eighths, order in PARTS]
    gather = Gather(sizes, parts, rows)
    weights = tap_weights(phases)
    scale = float(patch_total * (count // VIS_DEV) * side * side)
    anywhere = pl.BlockSpec(memory_space=pl.ANY)
    vmem = pl.BlockSpec(memory_space=pltpu.VMEM)
    smem = pl.BlockSpec(memory_space=pltpu.SMEM)
    lanes = VIS_DEV * TROWS
    dma = pltpu.SemaphoreType.DMA
    diff, table, left, vcol = pl.pallas_call(
        functools.partial(fit_kernel, gather, patch_total, scale),
        out_shape=(
            jax.ShapeDtypeStruct(pieces.shape, f32),
            jax.ShapeDtypeStruct((VIS_DEV, TROWS, TROWS), f32),
            jax.ShapeDtypeStruct((count, side, 4 * TROWS), bf16),
            jax.ShapeDtypeStruct((count, TROWS, side), f32),
        ),
        in_specs=[anywhere, anywhere, smem, smem, smem, smem, smem],
        out_specs=(anywhere, vmem, anywhere, anywhere),
        scratch_shapes=[
            pltpu.VMEM((count, side, side), f32),
            pltpu.VMEM((patch_total, side, side), f32),
            pltpu.VMEM((side + BLOCK, side), bf16),
            pltpu.VMEM((side + BLOCK, side), bf16),
            pltpu.VMEM((2 * BLOCK, 2 * BLOCK), bf16),
            pltpu.VMEM((side, side), bf16),
            pltpu.VMEM((side, side), bf16),
            pltpu.VMEM((count, TROWS, side), f32),
            pltpu.VMEM((count, TROWS, side), f32),
            pltpu.VMEM((count, side, 4 * TROWS), bf16),
            pltpu.VMEM((count, side, lanes), bf16),
            pltpu.VMEM((count, side, lanes), bf16),
            pltpu.VMEM((TROWS, lanes), f32),
            pltpu.VMEM((patch_total, TROWS, lanes), f32),
            dma((count,)),
            dma((count,)),
            dma((2,)),
            dma,
            dma((gather.sends,)),
            dma((len(parts) * gather.chips,)),
            dma((len(parts) * gather.chips,)),
            dma((patch_total,)),
            dma((patch_total,)),
        ],
        compiler_params=pltpu.CompilerParams(
            collective_id=0, has_side_effects=True, vmem_limit_bytes=60 * 2**20
        ),
        name="gather_warp_project",
    )(pieces, ref_patch, anchors.T, piece_patch, piece_visit, shifts.T, weights)
    matched = pl.pallas_call(
        subtract_kernel,
        out_shape=jax.ShapeDtypeStruct(pieces.shape, f32),
        grid=(count,),
        in_specs=[
            smem,
            pl.BlockSpec((1, side, side), lambda k: (k, 0, 0)),
            pl.BlockSpec((VIS_DEV, TROWS, TROWS), lambda k: (0, 0, 0)),
            pl.BlockSpec((1, side, 4 * TROWS), lambda k: (k, 0, 0)),
            pl.BlockSpec((count, TROWS, side), lambda k: (0, 0, 0)),
        ],
        out_specs=pl.BlockSpec((1, side, side), lambda k: (k, 0, 0)),
        scratch_shapes=[pltpu.VMEM((2, 4 * TROWS, side), bf16)],
        compiler_params=pltpu.CompilerParams(vmem_limit_bytes=60 * 2**20),
        name="subtract_fit",
    )(piece_visit, diff, table, left, vcol)
    return matched, table[:, :TERMS, :TERMS]


def solution(mesh):
    return jax.shard_map(
        functools.partial(body, mesh.shape["visit"]),
        mesh=mesh,
        in_specs=(
            P(("visit", "patch"), None, None),
            P("patch", "visit", None),
            P(("visit", "patch")),
            P(("visit", "patch")),
            P(("visit", "patch"), None),
            P(("visit", "patch"), None),
            P(("visit", "patch"), None),
        ),
        out_specs=(P(("visit", "patch"), None, None), P("visit", None, None)),
        check_vma=False,
    )
```
